32 devices in a mesh: dp: 8 (over z, x), tensor: 4 (over y, core).
Axes of the slice: x: 2, y: 2, z: 4, core: 2. Of those that a mesh axis runs over, the one named last changes fastest.
Arguments:
- activations: bfloat16 [4, 4096, 14336], P(None, 'dp', 'tensor'), may hold values from -6 to 6
- out_grads: bfloat16 [4, 4096, 4096], P(None, 'dp', 'tensor'), may hold values from -6 to 6
- proj_in: bfloat16 [4, 40, 14336], P(None, None, 'tensor'), may hold values from -0.046875 to 0.046875
- proj_out: bfloat16 [4, 40, 4096], P(None, None, 'tensor'), may hold values from -0.09375 to 0.09375
- lengths: int32 [32], P('dp'), may hold values from 16 to 128
- example_ids: int32 [32], P('dp'), may hold values from 0 to 31, each once
- prior_cov: bfloat16 [4, 1600, 1600], P('tensor'), as said below
- damping: float32 [4], P('tensor'), may hold values from 10 to 100
- queries: float32 [4, 64, 1600], P('tensor'), may hold values from -2 to 2
Outputs:
- scores: float32 [32, 64], P('dp')
The draws below stay inside these ranges and needn't reach their ends.
Inputs may be any that keep to these rules, and one draw needn't show every extreme that they name: Each slot's tokens at positions from lengths on are padding. `example_ids`: a permutation of the examples over the slots. `prior_cov`: symmetric and positive definite.
All inputs are finite; a program needn't handle non-finite values.
Results may differ from the reference program's by a relative error of at most 0.0003.
Values sent between devices are 32-bit elements; how exact they have to be, the bound alone decides.
A program may use at most 128 MiB of HBM per device.

```python
import math
import jax
import jax.numpy as jnp
from jax import lax

D = 4096
FF = 14336
KP = 40
SEQ = 128
NQ = 64
PROJ = 1600
LAYERS = 4
EXAMPLES = 32
TOKENS = 4096


def draw_prior_cov(key, part):
    spread = 120.0 / PROJ

    def one_layer(layer_key):
        raw_values = jax.random.uniform(layer_key, (PROJ, PROJ), jnp.float32, -spread, spread)
        symmetric = 0.5 * (raw_values + raw_values.T)
        identity = jnp.eye(PROJ, dtype=jnp.float32)
        off_diag = symmetric * (1.0 - identity)
        row_abs = jnp.sum(jnp.abs(off_diag), axis=1)
        return (off_diag + identity * (1.5 * row_abs[:, None] + 1.0)).astype(jnp.bfloat16)
    layer_keys = jax.random.split(jax.random.fold_in(key, 17), LAYERS)
    return jax.vmap(one_layer)(layer_keys)


def with_ends(values, rng, least, top_value):
    spot = [jax.random.randint(jax.random.fold_in(rng, axis), (), 0, length) for axis, length in enumerate(values.shape)]
    widest = values.shape.index(max(values.shape))
    neighbour = spot[:widest] + [(spot[widest] + 1) % values.shape[widest]] + spot[widest + 1:]
    return values.at[tuple(spot)].set(least).at[tuple(neighbour)].set(top_value)


def block_scale(own_key, shape, cuts, low, high):
    loudness = 1.0
    for position, parts in cuts:
        heights = jax.random.uniform(jax.random.fold_in(jax.random.fold_in(own_key, 6), position), (parts,), jnp.float32, low / len(cuts), high / len(cuts))
        loudness = loudness * jnp.repeat(jnp.exp(heights), shape[position] // parts).reshape((-1,) + (1,) * (len(shape) - 1 - position))
    return loudness


def bell_draw(rng, shape, deviation, reach, pieces=(), held_as=jnp.bfloat16):
    values = deviation * jax.random.normal(rng, shape, jnp.float32)
    if pieces:
        values = values * block_scale(rng, shape, pieces, -0.22, 0.18)
    return jnp.clip(values, -reach, reach).astype(held_as)


def setup_inputs(seed: int = 0) -> dict:
    key_list = jax.random.split(jax.random.key(seed), 10)
    activations = bell_draw(key_list[0], (LAYERS, TOKENS, FF), 1.0, 6.0, ((1, 8), (2, 4)))
    out_grads = bell_draw(key_list[1], (LAYERS, TOKENS, D), 1.0, 6.0, ((1, 8), (2, 4)))
    proj_in = bell_draw(key_list[2], (LAYERS, KP, FF), FF ** -0.5, 0.046875, ((2, 4),))
    proj_out = bell_draw(key_list[3], (LAYERS, KP, D), D ** -0.5, 0.09375, ((2, 4),))
    lengths = with_ends(jax.random.randint(key_list[4], (EXAMPLES,), SEQ // 8, SEQ + 1), jax.random.fold_in(key_list[4], 1), SEQ // 8, SEQ).astype(jnp.int32)
    example_ids = jax.random.permutation(key_list[5], EXAMPLES).astype(jnp.int32)
    prior_cov = draw_prior_cov(jax.random.fold_in(key_list[9], 71), 0)
    damping = jnp.clip(jnp.exp(math.log(100.0) - 2.3025851 * jax.random.uniform(key_list[7], (LAYERS,), jnp.float32) ** block_scale(key_list[7], (LAYERS,), ((0, 4),), -0.2, 0.2)), 10.0, 100.0)
    queries = bell_draw(key_list[8], (LAYERS, NQ, PROJ), 0.3, 2.0, ((0, 4),), jnp.float32)
    return dict(activations=activations, out_grads=out_grads, proj_in=proj_in, proj_out=proj_out, lengths=lengths, example_ids=example_ids, prior_cov=prior_cov, damping=damping, queries=queries)


def reference(activations, out_grads, proj_in, proj_out, lengths, example_ids, prior_cov, damping, queries):
    live_mask = (jnp.arange(SEQ, dtype=jnp.int32)[None, :] < lengths[:, None]).astype(jnp.float32)
    slot_scores = jnp.zeros((EXAMPLES, NQ), jnp.float32)
    for layer_index in range(LAYERS):
        in_rows = jnp.dot(activations[layer_index].astype(jnp.float32), proj_in[layer_index].T.astype(jnp.float32), preferred_element_type=jnp.float32)
        out_rows = jnp.dot(out_grads[layer_index].astype(jnp.float32), proj_out[layer_index].T.astype(jnp.float32), preferred_element_type=jnp.float32)
        in_rows = in_rows.reshape(EXAMPLES, SEQ, KP) * live_mask[:, :, None]
        out_rows = out_rows.reshape(EXAMPLES, SEQ, KP)
        proj_grads = jnp.einsum('est,esu->etu', out_rows, in_rows, precision=lax.Precision.HIGHEST).reshape(EXAMPLES, PROJ)
        moment = jnp.dot(proj_grads.T, proj_grads, precision=lax.Precision.HIGHEST)
        covariance = prior_cov[layer_index].astype(jnp.float32) + moment / EXAMPLES + damping[layer_index] * jnp.eye(PROJ, dtype=jnp.float32)
        factor_lower = jnp.linalg.cholesky(covariance)
        forward_part = lax.linalg.triangular_solve(factor_lower, queries[layer_index].T, left_side=True, lower=True)
        solved = lax.linalg.triangular_solve(factor_lower, forward_part, left_side=True, lower=True, transpose_a=True)
        slot_scores = slot_scores + jnp.dot(proj_grads, solved, precision=lax.Precision.HIGHEST)
    return jnp.zeros((EXAMPLES, NQ), jnp.float32).at[example_ids].set(slot_scores)
```

```python
import functools

import jax
import jax.numpy as jnp
from jax import lax
from jax.experimental import pallas as pl
from jax.experimental.pallas import tpu as pltpu
from jax.sharding import PartitionSpec as P

NB = 128
CB = 256


def round_up(value, step):
    return -(-value // step) * step


def split3(x):
    high = x.astype(jnp.bfloat16)
    rest = x - high.astype(jnp.float32)
    mid = rest.astype(jnp.bfloat16)
    low = (rest - mid.astype(jnp.float32)).astype(jnp.bfloat16)
    return high, mid, low


def stack_left(x):
    h, m, l = split3(x)
    return jnp.concatenate([h, h, m, h, l, m], axis=1)


def stack_right(x):
    h, m, l = split3(x)
    return jnp.concatenate([h, m, h, l, h, m], axis=1)


def dot_nt(a, b):
    return lax.dot_general(a, b, (((1,), (1,)), ((), ())), preferred_element_type=jnp.float32)


def across(row, shape=(8, NB)):
    return jnp.broadcast_to(row, shape)


def invert_block(rows):
    sub = lax.broadcasted_iota(jnp.int32, (8, NB), 0)
    lane = lax.broadcasted_iota(jnp.int32, (8, NB), 1)
    count = len(rows)
    for kb in range(count):
        base = 8 * kb
        strip = rows[kb]
        cols = [across(strip[:, base + j : base + j + 1]) for j in range(8)]
        for p in range(8):
            pivot_col = cols[p]
            inv = 1.0 / across(pivot_col[p : p + 1, :])
            new = []
            for j in range(8):
                if j == p:
                    new.append(jnp.where(sub == p, inv, -pivot_col * inv))
                else:
                    lead = across(cols[j][p : p + 1, :])
                    new.append(jnp.where(sub == p, lead * inv, cols[j] - (pivot_col * lead) * inv))
            cols = new
        inside = (lane >= base) & (lane < base + 8)
        strip = jnp.where(inside, jnp.where(lane - base == sub, 1.0, 0.0), strip)
        terms = [cols[j] * across(strip[j : j + 1, :]) for j in range(8)]
        top = ((terms[0] + terms[1]) + (terms[2] + terms[3])) + (
            (terms[4] + terms[5]) + (terms[6] + terms[7])
        )
        spread = [across(top[j : j + 1, :]) for j in range(8)]
        for step in range(1, count):
            i = (kb + step) % count
            row = rows[i]
            parts = [across(row[:, base + j : base + j + 1]) * spread[j] for j in range(8)]
            total = ((parts[0] + parts[1]) + (parts[2] + parts[3])) + (
                (parts[4] + parts[5]) + (parts[6] + parts[7])
            )
            rows[i] = jnp.where(inside, 0.0, row) - total
        rows[kb] = top
    return rows


def solve_kernel(
    size, damping_ref, prior_ref, rhs_ref, lead_ref, out_ref, mat, left, right, dinv
):
    width = rhs_ref.shape[1]
    col_blocks = width // CB
    all_blocks = mat.shape[0]
    slots = lead_ref.shape[2]
    damp = damping_ref[0, 0]

    def fill(i, carry):
        at = pl.multiple_of(i * 16, 16)
        row_id = lax.broadcasted_iota(jnp.int32, (16, CB), 0) + at
        col_id = lax.broadcasted_iota(jnp.int32, (16, CB), 1)
        for jj in range(col_blocks):
            lo, hi = jj * CB, min((jj + 1) * CB, size)
            piece = prior_ref[pl.ds(at, 16), lo:hi].astype(jnp.float32)
            if hi - lo < CB:
                piece = jnp.concatenate(
                    [piece, jnp.zeros((16, CB - (hi - lo)), jnp.float32)], axis=1
                )
            piece = jnp.where(row_id == col_id + lo, piece + damp, piece)
            mat[jj, pl.ds(at, 16), :] = piece
        return carry

    lax.fori_loop(0, size // 16, fill, 0)
    for jj in range(col_blocks):
        row_id = lax.broadcasted_iota(jnp.int32, (width - size, CB), 0) + size
        col_id = lax.broadcasted_iota(jnp.int32, (width - size, CB), 1) + jj * CB
        mat[jj, size:width, :] = jnp.where(row_id == col_id, 1.0, 0.0)
        mat[jj, width:, :] = rhs_ref[:, jj * CB : (jj + 1) * CB]
    mat[col_blocks, width:, :] = jnp.zeros((mat.shape[1] - width, CB), jnp.float32)

    def trail(first):
        def per_col(jj, carry):
            weights = right[pl.ds(pl.multiple_of(jj * CB, CB), CB), :]

            def per_row(r, inner):
                at = pl.multiple_of(r * CB, CB)
                mat[jj, pl.ds(at, CB), :] -= dot_nt(left[pl.ds(at, CB), :], weights)
                return inner

            return lax.fori_loop(jj, all_blocks, per_row, carry)

        lax.fori_loop(first, all_blocks, per_col, 0)

    def lead_rows(r, carry):
        at = pl.multiple_of(r * CB, CB)
        piece = lead_ref[0, pl.ds(at, CB), :]
        right[pl.ds(at, CB), :] = stack_right(piece)
        left[pl.ds(at, CB), :] = stack_left(lead_ref[1, pl.ds(at, CB), :])
        return carry

    lax.fori_loop(0, all_blocks, lead_rows, 0)
    trail(0)

    def step(k, carry):
        half = k // 2
        lanes = pl.ds(pl.multiple_of((k % 2) * NB, NB), NB)
        top = pl.multiple_of(k * NB, NB)
        rows = [mat[half, pl.ds(top + 8 * i, 8), lanes] for i in range(NB // 8)]
        rows = invert_block(rows)
        for i in range(NB // 8):
            dinv[8 * i : 8 * i + 8, :] = rows[i]
        inverse = stack_right(dinv[...])

        def per_row(r, inner):
            at = pl.multiple_of(r * CB, CB)
            panel = mat[half, pl.ds(at, CB), lanes]
            right[pl.ds(at, CB), :] = stack_right(panel)
            left[pl.ds(at, CB), :] = stack_left(dot_nt(stack_left(panel), inverse))
            return inner

        lax.fori_loop(half, all_blocks, per_row, 0)
        trail((k + 1) // 2)
        return carry

    lax.fori_loop(0, round_up(size, NB) // NB, step, 0)
    out_ref[...] = -mat[col_blocks, width:, :]


def solve_scores(prior, damping, queries, grads):
    slots, size = grads.shape
    asked = queries.shape[0]
    width = round_up(size, CB)
    extra = CB
    rows = width + extra
    rhs = jnp.concatenate([grads, queries], axis=0)
    rhs = jnp.pad(rhs, ((0, extra - slots - asked), (0, width - size)))
    lead = jnp.pad(grads.T, ((0, rows - size), (0, NB - slots)))
    lead = jnp.stack([lead, lead * (-1.0 / slots)])
    out = pl.pallas_call(
        functools.partial(solve_kernel, size),
        out_shape=jax.ShapeDtypeStruct((extra, CB), jnp.float32),
        in_specs=[
            pl.BlockSpec(memory_space=pltpu.SMEM),
            pl.BlockSpec(memory_space=pltpu.VMEM),
            pl.BlockSpec(memory_space=pltpu.VMEM),
            pl.BlockSpec(memory_space=pltpu.VMEM),
        ],
        out_specs=pl.BlockSpec(memory_space=pltpu.VMEM),
        scratch_shapes=[
            pltpu.VMEM((rows // CB, rows, CB), jnp.float32),
            pltpu.VMEM((rows, 6 * NB), jnp.bfloat16),
            pltpu.VMEM((rows, 6 * NB), jnp.bfloat16),
            pltpu.VMEM((NB, NB), jnp.float32),
        ],
        compiler_params=pltpu.CompilerParams(vmem_limit_bytes=56 * 1024 * 1024),
    )(damping.reshape(1, 1), prior, rhs, lead)
    return out[:slots, slots : slots + asked]


def per_device(
    activations, out_grads, proj_in, proj_out, lengths, example_ids, prior_cov, damping, queries
):
    ex_local = lengths.shape[0]
    rank = proj_in.shape[1]
    seq_len = activations.shape[1] // ex_local
    owner_index = lax.axis_index("tensor")
    live_mask = (jnp.arange(seq_len, dtype=jnp.int32)[None, :] < lengths[:, None]).astype(
        jnp.float32
    )
    in_parts = jnp.einsum("ltf,lkf->ltk", activations, proj_in, preferred_element_type=jnp.float32)
    out_parts = jnp.einsum("ltf,lkf->ltk", out_grads, proj_out, preferred_element_type=jnp.float32)
    in_summed, out_summed = lax.psum((in_parts, out_parts), "tensor")
    in_rows = lax.dynamic_index_in_dim(in_summed, owner_index, 0, keepdims=False)
    out_rows = lax.dynamic_index_in_dim(out_summed, owner_index, 0, keepdims=False)
    in_rows = in_rows.reshape(ex_local, seq_len, rank) * live_mask[:, :, None]
    out_rows = out_rows.reshape(ex_local, seq_len, rank)
    proj_grads = jnp.einsum(
        "est,esu->etu", out_rows, in_rows, precision=lax.Precision.HIGHEST
    ).reshape(ex_local, rank * rank)
    ids = lax.all_gather(example_ids, "dp", axis=0, tiled=True)
    piece_rows = lax.all_gather(proj_grads, "dp", axis=0, tiled=True)
    scores = solve_scores(prior_cov[0], damping, queries[0], piece_rows)
    mine = lax.axis_index("dp") * ex_local + jnp.arange(ex_local, dtype=jnp.int32)
    pick = (ids[None, :] == mine[:, None]).astype(jnp.float32)
    chosen = jnp.dot(pick, scores, precision=lax.Precision.HIGHEST)
    return lax.psum(chosen, "tensor")


def solution(mesh):
    in_specs = (
        P(None, "dp", "tensor"),
        P(None, "dp", "tensor"),
        P(None, None, "tensor"),
        P(None, None, "tensor"),
        P("dp"),
        P("dp"),
        P("tensor", None, None),
        P("tensor"),
        P("tensor", None, None),
    )
    out_specs = P("dp", None)
    return jax.shard_map(
        per_device, mesh=mesh, in_specs=in_specs, out_specs=out_specs, check_vma=False
    )
```

```python
import functools

import jax
import jax.numpy as jnp
from jax import lax
from jax.experimental import pallas as pl
from jax.experimental.pallas import tpu as pltpu
from jax.sharding import PartitionSpec as P

MESH = pl.DeviceIdType.MESH
NB = 128
CB = 256
TERMS = 6


def round_up(value, step):
    return -(-value // step) * step


def split3(x):
    high = x.astype(jnp.bfloat16)
    rest = x - high.astype(jnp.float32)
    mid = rest.astype(jnp.bfloat16)
    low = (rest - mid.astype(jnp.float32)).astype(jnp.bfloat16)
    return high, mid, low


def stack_left(x):
    h, m, l = split3(x)
    return jnp.concatenate([h, h, m, h, l, m], axis=1)


def stack_right(x):
    h, m, l = split3(x)
    return jnp.concatenate([h, m, h, l, h, m], axis=1)


def dot_nt(a, b):
    return lax.dot_general(a, b, (((1,), (1,)), ((), ())), preferred_element_type=jnp.float32)


def across(row, shape=(8, NB)):
    return jnp.broadcast_to(row, shape)


def invert_block(rows):
    sub = lax.broadcasted_iota(jnp.int32, (8, NB), 0)
    lane = lax.broadcasted_iota(jnp.int32, (8, NB), 1)
    count = len(rows)
    for kb in range(count):
        base = 8 * kb
        strip = rows[kb]
        cols = [across(strip[:, base + j : base + j + 1]) for j in range(8)]
        for p in range(8):
            pivot_col = cols[p]
            inv = 1.0 / across(pivot_col[p : p + 1, :])
            new = []
            for j in range(8):
                if j == p:
                    new.append(jnp.where(sub == p, inv, -pivot_col * inv))
                else:
                    lead = across(cols[j][p : p + 1, :])
                    new.append(jnp.where(sub == p, lead * inv, cols[j] - (pivot_col * lead) * inv))
            cols = new
        inside = (lane >= base) & (lane < base + 8)
        strip = jnp.where(inside, jnp.where(lane - base == sub, 1.0, 0.0), strip)
        terms = [cols[j] * across(strip[j : j + 1, :]) for j in range(8)]
        top = ((terms[0] + terms[1]) + (terms[2] + terms[3])) + (
            (terms[4] + terms[5]) + (terms[6] + terms[7])
        )
        spread = [across(top[j : j + 1, :]) for j in range(8)]
        for step in range(1, count):
            i = (kb + step) % count
            row = rows[i]
            parts = [across(row[:, base + j : base + j + 1]) * spread[j] for j in range(8)]
            total = ((parts[0] + parts[1]) + (parts[2] + parts[3])) + (
                (parts[4] + parts[5]) + (parts[6] + parts[7])
            )
            rows[i] = jnp.where(inside, 0.0, row) - total
        rows[kb] = top
    return rows


def solve_kernel(
    size, slots, asked, ex_local, damping_ref, prior_ref, rhs_ref, out_ref, mat, left, right, dinv
):
    width = rhs_ref.shape[1]
    col_blocks = width // CB
    all_blocks = mat.shape[0]
    damp = damping_ref[0, 0]

    def fill(i, carry):
        at = pl.multiple_of(i * 16, 16)
        row_id = lax.broadcasted_iota(jnp.int32, (16, CB), 0) + at
        col_id = lax.broadcasted_iota(jnp.int32, (16, CB), 1)
        for jj in range(col_blocks):
            lo, hi = jj * CB, min((jj + 1) * CB, size)
            piece = prior_ref[pl.ds(at, 16), lo:hi].astype(jnp.float32)
            if hi - lo < CB:
                piece = jnp.concatenate(
                    [piece, jnp.zeros((16, CB - (hi - lo)), jnp.float32)], axis=1
                )
            piece = jnp.where(row_id == col_id + lo, piece + damp, piece)
            mat[jj, pl.ds(at, 16), :] = piece
        return carry

    lax.fori_loop(0, size // 16, fill, 0)
    for jj in range(col_blocks):
        row_id = lax.broadcasted_iota(jnp.int32, (width - size, CB), 0) + size
        col_id = lax.broadcasted_iota(jnp.int32, (width - size, CB), 1) + jj * CB
        mat[jj, size:width, :] = jnp.where(row_id == col_id, 1.0, 0.0)
        mat[jj, width:, :] = rhs_ref[:, jj * CB : (jj + 1) * CB]
    mat[col_blocks, width:, :] = jnp.zeros((mat.shape[1] - width, CB), jnp.float32)

    def trail(first):
        def per_col(jj, carry):
            weights = right[pl.ds(pl.multiple_of(jj * CB, CB), CB), :]

            def per_row(r, inner):
                at = pl.multiple_of(r * CB, CB)
                mat[jj, pl.ds(at, CB), :] -= dot_nt(left[pl.ds(at, CB), :], weights)
                return inner

            return lax.fori_loop(jj, all_blocks, per_row, carry)

        lax.fori_loop(first, all_blocks, per_col, 0)

    live = lax.broadcasted_iota(jnp.int32, (NB, CB), 0) < slots
    for jj in range(col_blocks):
        piece = jnp.where(live, rhs_ref[0:NB, jj * CB : (jj + 1) * CB], 0.0).T
        right[jj * CB : (jj + 1) * CB, :] = stack_right(piece)
        left[jj * CB : (jj + 1) * CB, :] = stack_left(piece * (-1.0 / slots))
    right[width:, :] = jnp.zeros((mat.shape[1] - width, TERMS * NB), jnp.bfloat16)
    left[width:, :] = jnp.zeros((mat.shape[1] - width, TERMS * NB), jnp.bfloat16)
    trail(0)

    def step(k, carry):
        half = k // 2
        lanes = pl.ds(pl.multiple_of((k % 2) * NB, NB), NB)
        top = pl.multiple_of(k * NB, NB)
        rows = [mat[half, pl.ds(top + 8 * i, 8), lanes] for i in range(NB // 8)]
        rows = invert_block(rows)
        for i in range(NB // 8):
            dinv[8 * i : 8 * i + 8, :] = rows[i]
        inverse = stack_right(dinv[...])

        def per_row(r, inner):
            at = pl.multiple_of(r * CB, CB)
            panel = mat[half, pl.ds(at, CB), lanes]
            right[pl.ds(at, CB), :] = stack_right(panel)
            left[pl.ds(at, CB), :] = stack_left(dot_nt(stack_left(panel), inverse))
            return inner

        lax.fori_loop(half, all_blocks, per_row, 0)
        trail((k + 1) // 2)
        return carry

    lax.fori_loop(0, round_up(size, NB) // NB, step, 0)
    id_at = round_up(size, NB)
    ids = jnp.broadcast_to(rhs_ref[0:slots, id_at : id_at + 1], (slots, NB))
    own = lax.broadcasted_iota(jnp.int32, (slots, NB), 1) + lax.axis_index("dp") * ex_local
    pick = jnp.where(ids == own.astype(jnp.float32), -1.0, 0.0)
    chosen = lax.dot_general(
        pick,
        mat[col_blocks, width : width + slots, :],
        (((0,), (0,)), ((), ())),
        precision=lax.Precision.HIGHEST,
        preferred_element_type=jnp.float32,
    )
    out_ref[...] = chosen[0:ex_local, slots : slots + asked]


def project_kernel(
    ex_local,
    size,
    act_hbm,
    og_hbm,
    pin_ref,
    pout_ref,
    aux_ref,
    query_ref,
    out_ref,
    act,
    og,
    part,
    got,
    mine,
    gathered,
    load_sem,
    part_send,
    part_recv,
    dp_send,
    dp_recv,
):
    layers = lax.axis_size("tensor")
    pieces = lax.axis_size("dp")
    ti = lax.axis_index("tensor")
    di = lax.axis_index("dp")
    rank = pin_ref.shape[1]
    tokens = act.shape[1]
    seq_len = tokens // ex_local
    half = mine.shape[1]

    loads = []
    for d in range(1, layers + 1):
        layer = lax.rem(ti + d, layers)
        one = pltpu.make_async_copy(act_hbm.at[layer], act.at[d - 1], load_sem.at[2 * d - 2])
        two = pltpu.make_async_copy(og_hbm.at[layer], og.at[d - 1], load_sem.at[2 * d - 1])
        one.start()
        two.start()
        loads.append((one, two))

    barrier = pltpu.get_barrier_semaphore()
    for d in range(1, layers):
        pl.semaphore_signal(
            barrier, inc=1, device_id=(di, lax.rem(ti + d, layers)), device_id_type=MESH
        )
    for d in range(1, pieces):
        pl.semaphore_signal(
            barrier, inc=1, device_id=(lax.rem(di + d, pieces), ti), device_id_type=MESH
        )
    pl.semaphore_wait(barrier, layers - 1 + pieces - 1)

    sends = []
    for d in range(1, layers + 1):
        layer = lax.rem(ti + d, layers)
        loads[d - 1][0].wait()
        loads[d - 1][1].wait()
        in_part = dot_nt(act[d - 1], pin_ref[layer])
        out_part = dot_nt(og[d - 1], pout_ref[layer])
        gap = jnp.zeros((tokens, NB // 2 - rank), jnp.float32)
        both = jnp.concatenate([in_part, gap, out_part, gap], axis=1).T
        part[d - 1, 0:rank, :] = both[0:rank]
        part[d - 1, rank : 2 * rank, :] = both[NB // 2 : NB // 2 + rank]
        if d < layers:
            copy = pltpu.make_async_remote_copy(
                src_ref=part.at[d - 1],
                dst_ref=got.at[d - 1],
                send_sem=part_send.at[d - 1],
                recv_sem=part_recv.at[d - 1],
                device_id=(di, layer),
                device_id_type=MESH,
            )
            copy.start()
            sends.append(copy)
    out_ref[...] = jnp.zeros_like(out_ref)
    total_slots = ex_local * pieces
    out_ref[total_slots : total_slots + query_ref.shape[0], 0:size] = query_ref[...]
    total = part[layers - 1]
    for d, copy in enumerate(sends):
        copy.wait()
        total = total + got[d]
    in_rows = total[0:rank] * aux_ref[0:1, :]
    out_rows = total[rank : 2 * rank]
    grads = []
    for s in range(ex_local):
        lanes = slice(s * seq_len, (s + 1) * seq_len)
        grads.append(
            lax.dot_general(
                out_rows[:, lanes],
                in_rows[:, lanes],
                (((1,), (1,)), ((), ())),
                precision=lax.Precision.HIGHEST,
                preferred_element_type=jnp.float32,
            )
        )
    stacked = jnp.concatenate(grads, axis=0)
    width = 2 * half
    col = lax.broadcasted_iota(jnp.int32, (rank, width), 1)
    row = lax.broadcasted_iota(jnp.int32, (rank, width), 0)
    colf = col.astype(jnp.float32)
    residue = colf - rank * jnp.floor((colf + 0.5) * (1.0 / rank))
    place = jnp.where(residue == row.astype(jnp.float32), 1.0, 0.0).astype(jnp.bfloat16)
    flat = None
    for term in split3(stacked):
        piece = jnp.dot(term, place, preferred_element_type=jnp.float32)
        flat = piece if flat is None else flat + piece
    keep = (col >= row * rank) & (col < row * rank + rank)
    id_col = lax.broadcasted_iota(jnp.int32, (1, width), 1) == round_up(size, NB)
    for s in range(ex_local):
        slot = jnp.where(keep, flat[s * rank : (s + 1) * rank], 0.0)
        line = jnp.sum(slot, axis=0, keepdims=True)
        line = jnp.where(id_col, jnp.broadcast_to(aux_ref[1:2, s : s + 1], line.shape), line)
        mine[s : s + 1, :] = line[:, 0:half]
        mine[ex_local + s : ex_local + s + 1, :] = line[:, half:width]
    copies = []
    for d in range(1, pieces):
        copy = pltpu.make_async_remote_copy(
            src_ref=mine,
            dst_ref=gathered.at[di],
            send_sem=dp_send.at[d - 1],
            recv_sem=dp_recv.at[d - 1],
            device_id=(lax.rem(di + d, pieces), ti),
            device_id_type=MESH,
        )
        copy.start()
        copies.append(copy)
    gathered[di] = mine[...]
    for copy in copies:
        copy.wait()
    for p in range(pieces):
        block = gathered[p]
        out_ref[p * ex_local : (p + 1) * ex_local, 0:half] = block[0:ex_local]
        out_ref[p * ex_local : (p + 1) * ex_local, half:width] = block[ex_local : 2 * ex_local]


def project(activations, out_grads, proj_in, proj_out, lengths, example_ids, queries):
    ex_local = lengths.shape[0]
    layers, tokens, _ = activations.shape
    rank = proj_in.shape[1]
    size = rank * rank
    width = round_up(size, CB)
    pieces = lax.axis_size("dp")
    seq_len = tokens // ex_local
    live = (jnp.arange(seq_len, dtype=jnp.int32)[None, :] < lengths[:, None]).astype(jnp.float32)
    ids = jnp.pad(example_ids.astype(jnp.float32), (0, tokens - ex_local))
    aux = jnp.stack([live.reshape(tokens), ids])
    return pl.pallas_call(
        functools.partial(project_kernel, ex_local, size),
        out_shape=jax.ShapeDtypeStruct((CB, width), jnp.float32),
        in_specs=[pl.BlockSpec(memory_space=pl.ANY)] * 2
        + [pl.BlockSpec(memory_space=pltpu.VMEM)] * 4,
        out_specs=pl.BlockSpec(memory_space=pltpu.VMEM),
        scratch_shapes=[
            pltpu.VMEM(activations.shape, activations.dtype),
            pltpu.VMEM(out_grads.shape, out_grads.dtype),
            pltpu.VMEM((layers, 2 * rank, tokens), jnp.float32),
            pltpu.VMEM((layers - 1, 2 * rank, tokens), jnp.float32),
            pltpu.VMEM((2 * ex_local, width // 2), jnp.float32),
            pltpu.VMEM((pieces, 2 * ex_local, width // 2), jnp.float32),
            pltpu.SemaphoreType.DMA((2 * layers,)),
            pltpu.SemaphoreType.DMA((layers - 1,)),
            pltpu.SemaphoreType.DMA((layers - 1,)),
            pltpu.SemaphoreType.DMA((pieces - 1,)),
            pltpu.SemaphoreType.DMA((pieces - 1,)),
        ],
        compiler_params=pltpu.CompilerParams(
            collective_id=0, has_side_effects=True, vmem_limit_bytes=48 * 1024 * 1024
        ),
    )(activations, out_grads, proj_in, proj_out, aux, queries)


def solve_scores(prior, damping, rhs, slots, asked, ex_local):
    size = prior.shape[0]
    width = rhs.shape[1]
    rows = width + rhs.shape[0]
    return pl.pallas_call(
        functools.partial(solve_kernel, size, slots, asked, ex_local),
        out_shape=jax.ShapeDtypeStruct((ex_local, asked), jnp.float32),
        in_specs=[
            pl.BlockSpec(memory_space=pltpu.SMEM),
            pl.BlockSpec(memory_space=pltpu.VMEM),
            pl.BlockSpec(memory_space=pltpu.VMEM),
        ],
        out_specs=pl.BlockSpec(memory_space=pltpu.VMEM),
        scratch_shapes=[
            pltpu.VMEM((rows // CB, rows, CB), jnp.float32),
            pltpu.VMEM((rows, TERMS * NB), jnp.bfloat16),
            pltpu.VMEM((rows, TERMS * NB), jnp.bfloat16),
            pltpu.VMEM((NB, NB), jnp.float32),
        ],
        compiler_params=pltpu.CompilerParams(vmem_limit_bytes=56 * 1024 * 1024),
    )(damping.reshape(1, 1), prior, rhs)


def per_device(
    activations, out_grads, proj_in, proj_out, lengths, example_ids, prior_cov, damping, queries
):
    ex_local = lengths.shape[0]
    slots = ex_local * lax.axis_size("dp")
    rhs = project(
        activations, out_grads, proj_in, proj_out, lengths, example_ids, queries[0]
    )
    chosen = solve_scores(prior_cov[0], damping, rhs, slots, queries.shape[1], ex_local)
    return lax.psum(chosen, "tensor")


def solution(mesh):
    in_specs = (
        P(None, "dp", "tensor"),
        P(None, "dp", "tensor"),
        P(None, None, "tensor"),
        P(None, None, "tensor"),
        P("dp"),
        P("dp"),
        P("tensor", None, None),
        P("tensor"),
        P("tensor", None, None),
    )
    out_specs = P("dp", None)
    return jax.shard_map(
        per_device, mesh=mesh, in_specs=in_specs, out_specs=out_specs, check_vma=False
    )
```

```python
import functools

import jax
import jax.numpy as jnp
from jax import lax
from jax.experimental import pallas as pl
from jax.experimental.pallas import tpu as pltpu
from jax.sharding import PartitionSpec as P

MESH = pl.DeviceIdType.MESH
NB = 128
CB = 256
TERMS = 4


def round_up(value, step):
    return -(-value // step) * step


def split3(x):
    high = x.astype(jnp.bfloat16)
    rest = x - high.astype(jnp.float32)
    mid = rest.astype(jnp.bfloat16)
    low = (rest - mid.astype(jnp.float32)).astype(jnp.bfloat16)
    return high, mid, low


def split2(x):
    high = x.astype(jnp.bfloat16)
    return high, (x - high.astype(jnp.float32)).astype(jnp.bfloat16)


def stack_left(x):
    h, m = split2(x)
    return jnp.concatenate([h, m, h, m], axis=1)


def stack_right(x):
    h, m = split2(x)
    return jnp.concatenate([h, h, m, m], axis=1)


def dot_nt(a, b):
    return lax.dot_general(a, b, (((1,), (1,)), ((), ())), preferred_element_type=jnp.float32)


def across(row, shape=(8, NB)):
    return jnp.broadcast_to(row, shape)


def invert_eight(cols):
    sub = lax.broadcasted_iota(jnp.int32, (8, NB), 0)
    for p in range(0, 8, 2):
        q = p + 1
        at_p, at_q = sub == p, sub == q
        first, second = cols[p], cols[q]
        a = across(first[p : p + 1, :])
        b = across(second[p : p + 1, :])
        c = across(second[q : q + 1, :])
        inv = 1.0 / (a * c - b * b)
        new = []
        for j in range(8):
            if j == p:
                new.append(jnp.where(at_p, c, jnp.where(at_q, -b, second * b - first * c)) * inv)
            elif j == q:
                new.append(jnp.where(at_p, -b, jnp.where(at_q, a, first * b - second * a)) * inv)
            else:
                u = across(cols[j][p : p + 1, :])
                v = across(cols[j][q : q + 1, :])
                x = c * u - b * v
                y = a * v - b * u
                change = jnp.where(at_p, -x, jnp.where(at_q, -y, first * x + second * y))
                new.append(jnp.where(at_p | at_q, 0.0, cols[j]) - change * inv)
        cols = new
    return cols


def tree_sum(terms):
    while len(terms) > 1:
        terms = [terms[i] + terms[i + 1] for i in range(0, len(terms), 2)]
    return terms[0]


def invert_block(rows, between):
    sub = lax.broadcasted_iota(jnp.int32, (8, NB), 0)
    lane = lax.broadcasted_iota(jnp.int32, (8, NB), 1)
    count = len(rows)
    diagonal = [jnp.where(lane == sub + 8 * i, rows[i], 0.0) for i in range(count)]
    along = lax.rsqrt(across(jnp.sum(tree_sum(diagonal), axis=0, keepdims=True)))
    down = [
        lax.rsqrt(jnp.broadcast_to(jnp.sum(d, axis=1, keepdims=True), (8, NB))) for d in diagonal
    ]
    rows = [rows[i] * down[i] * along for i in range(count)]
    for kb in range(count):
        base = 8 * kb
        strip = rows[kb]
        cols = invert_eight([across(strip[:, base + j : base + j + 1]) for j in range(8)])
        inside = (lane >= base) & (lane < base + 8)
        strip = jnp.where(inside, jnp.where(lane - base == sub, 1.0, 0.0), strip)
        top = tree_sum([cols[j] * across(strip[j : j + 1, :]) for j in range(8)])
        spread = [across(top[j : j + 1, :]) for j in range(8)]
        for step in range(1, count):
            i = (kb + step) % count
            row = rows[i]
            parts = [across(row[:, base + j : base + j + 1]) * spread[j] for j in range(8)]
            rows[i] = jnp.where(inside, 0.0, row) - tree_sum(parts)
        rows[kb] = top
        between()
    return [rows[i] * down[i] * along for i in range(count)]


def tiles_each(k, all_blocks):
    rest = all_blocks - 1 - (k + 1) // 2
    return -(-(rest * (rest + 1) // 2) // (NB // 8))


def solve_kernel(
    size, slots, asked, ex_local, damping_ref, prior_ref, rhs_ref, out_ref, mat, left, right, dinv
):
    width = rhs_ref.shape[1]
    col_blocks = width // CB
    all_blocks = mat.shape[0]
    damp = damping_ref[0, 0]

    def fill(i, carry):
        at = pl.multiple_of(i * 16, 16)
        row_id = lax.broadcasted_iota(jnp.int32, (16, CB), 0) + at
        col_id = lax.broadcasted_iota(jnp.int32, (16, CB), 1)
        for jj in range(col_blocks):
            lo, hi = jj * CB, min((jj + 1) * CB, size)
            piece = prior_ref[pl.ds(at, 16), lo:hi].astype(jnp.float32)
            if hi - lo < CB:
                piece = jnp.concatenate(
                    [piece, jnp.zeros((16, CB - (hi - lo)), jnp.float32)], axis=1
                )
            piece = jnp.where(row_id == col_id + lo, piece + damp, piece)
            mat[jj, pl.ds(at, 16), :] = piece
        return carry

    lax.fori_loop(0, size // 16, fill, 0)
    for jj in range(col_blocks):
        row_id = lax.broadcasted_iota(jnp.int32, (width - size, CB), 0) + size
        col_id = lax.broadcasted_iota(jnp.int32, (width - size, CB), 1) + jj * CB
        mat[jj, size:width, :] = jnp.where(row_id == col_id, 1.0, 0.0)
        mat[jj, width:, :] = rhs_ref[:, jj * CB : (jj + 1) * CB]
    mat[col_blocks, width:, :] = jnp.zeros((mat.shape[1] - width, CB), jnp.float32)

    def tile(jj, r):
        at = pl.multiple_of(r * CB, CB)
        weights = right[pl.ds(pl.multiple_of(jj * CB, CB), CB), :]
        mat[jj, pl.ds(at, CB), :] -= dot_nt(left[pl.ds(at, CB), :], weights)

    def update_col(jj):
        def per_row(r, carry):
            tile(jj, r)
            return carry

        lax.fori_loop(jj, all_blocks, per_row, 0)

    live = lax.broadcasted_iota(jnp.int32, (NB, CB), 0) < slots
    for jj in range(col_blocks):
        piece = jnp.where(live, rhs_ref[0:NB, jj * CB : (jj + 1) * CB], 0.0).T
        right[jj * CB : (jj + 1) * CB, :] = stack_right(piece)
        left[jj * CB : (jj + 1) * CB, :] = stack_left(piece * (-1.0 / slots))
    right[width:, :] = jnp.zeros((mat.shape[1] - width, TERMS * NB), jnp.bfloat16)
    left[width:, :] = jnp.zeros((mat.shape[1] - width, TERMS * NB), jnp.bfloat16)
    def panels(k):
        half = k // 2
        lanes = pl.ds(pl.multiple_of((k % 2) * NB, NB), NB)
        inverse = stack_right(dinv[...])

        def per_row(r, carry):
            at = pl.multiple_of(r * CB, CB)
            panel = mat[half, pl.ds(at, CB), lanes]
            right[pl.ds(at, CB), :] = stack_right(panel)
            left[pl.ds(at, CB), :] = stack_left(dot_nt(stack_left(panel), inverse))
            return carry

        lax.fori_loop(half, all_blocks, per_row, 0)

    def step(each, k, carry):
        @pl.when(k >= 0)
        def _():
            panels(k)

        later = k + 1
        half = later // 2
        update_col(half)
        lanes = pl.ds(pl.multiple_of((later % 2) * NB, NB), NB)
        top = pl.multiple_of(later * NB, NB)
        rows = [mat[half, pl.ds(top + 8 * i, 8), lanes] for i in range(NB // 8)]
        place = [half + 1, half + 1]

        def between():
            for _ in range(each):
                jj, r = place
                left_over = jj < all_blocks
                tile(jnp.where(left_over, jj, all_blocks - 1), jnp.where(left_over, r, 0))
                wrap = r + 1 >= all_blocks
                place[0] = jnp.where(wrap, jj + 1, jj)
                place[1] = jnp.where(wrap, jj + 1, r + 1)

        rows = invert_block(rows, between)
        for i in range(NB // 8):
            dinv[8 * i : 8 * i + 8, :] = rows[i]
        return carry

    blocks = round_up(size, NB) // NB
    start = -1
    while start < blocks - 1:
        each = tiles_each(start, all_blocks)
        stop = start
        while stop < blocks - 1 and tiles_each(stop, all_blocks) == each:
            stop += 1
        lax.fori_loop(start, stop, functools.partial(step, each), 0)
        start = stop
    panels(blocks - 1)
    for jj in range(blocks // 2, all_blocks):
        update_col(jj)
    id_at = round_up(size, NB)
    ids = jnp.broadcast_to(rhs_ref[0:slots, id_at : id_at + 1], (slots, NB))
    own = lax.broadcasted_iota(jnp.int32, (slots, NB), 1) + lax.axis_index("dp") * ex_local
    pick = jnp.where(ids == own.astype(jnp.float32), -1.0, 0.0)
    chosen = lax.dot_general(
        pick,
        mat[col_blocks, width : width + slots, :],
        (((0,), (0,)), ((), ())),
        precision=lax.Precision.HIGHEST,
        preferred_element_type=jnp.float32,
    )
    out_ref[...] = chosen[0:ex_local, slots : slots + asked]


def project_kernel(
    ex_local,
    size,
    act_hbm,
    og_hbm,
    pin_ref,
    pout_ref,
    aux_ref,
    query_ref,
    out_ref,
    act,
    og,
    part,
    got,
    mine,
    gathered,
    load_sem,
    part_send,
    part_recv,
    dp_send,
    dp_recv,
):
    layers = lax.axis_size("tensor")
    pieces = lax.axis_size("dp")
    ti = lax.axis_index("tensor")
    di = lax.axis_index("dp")
    rank = pin_ref.shape[1]
    tokens = act.shape[1]
    seq_len = tokens // ex_local
    half = mine.shape[1]

    loads = []
    for d in range(1, layers + 1):
        layer = lax.rem(ti + d, layers)
        one = pltpu.make_async_copy(act_hbm.at[layer], act.at[d - 1], load_sem.at[2 * d - 2])
        two = pltpu.make_async_copy(og_hbm.at[layer], og.at[d - 1], load_sem.at[2 * d - 1])
        one.start()
        two.start()
        loads.append((one, two))

    barrier = pltpu.get_barrier_semaphore()
    for d in range(1, layers):
        pl.semaphore_signal(
            barrier, inc=1, device_id=(di, lax.rem(ti + d, layers)), device_id_type=MESH
        )
    for d in range(1, pieces):
        pl.semaphore_signal(
            barrier, inc=1, device_id=(lax.rem(di + d, pieces), ti), device_id_type=MESH
        )
    pl.semaphore_wait(barrier, layers - 1 + pieces - 1)

    sends = []
    for d in range(1, layers + 1):
        layer = lax.rem(ti + d, layers)
        loads[d - 1][0].wait()
        loads[d - 1][1].wait()
        in_part = dot_nt(act[d - 1], pin_ref[layer])
        out_part = dot_nt(og[d - 1], pout_ref[layer])
        gap = jnp.zeros((tokens, NB // 2 - rank), jnp.float32)
        both = jnp.concatenate([in_part, gap, out_part, gap], axis=1).T
        part[d - 1, 0:rank, :] = both[0:rank]
        part[d - 1, rank : 2 * rank, :] = both[NB // 2 : NB // 2 + rank]
        if d < layers:
            copy = pltpu.make_async_remote_copy(
                src_ref=part.at[d - 1],
                dst_ref=got.at[d - 1],
                send_sem=part_send.at[d - 1],
                recv_sem=part_recv.at[d - 1],
                device_id=(di, layer),
                device_id_type=MESH,
            )
            copy.start()
            sends.append(copy)
    out_ref[...] = jnp.zeros_like(out_ref)
    total_slots = ex_local * pieces
    out_ref[total_slots : total_slots + query_ref.shape[0], 0:size] = query_ref[...]
    total = part[layers - 1]
    for d, copy in enumerate(sends):
        copy.wait()
        total = total + got[d]
    in_rows = total[0:rank] * aux_ref[0:1, :]
    out_rows = total[rank : 2 * rank]
    grads = []
    for s in range(ex_local):
        lanes = slice(s * seq_len, (s + 1) * seq_len)
        grads.append(
            lax.dot_general(
                out_rows[:, lanes],
                in_rows[:, lanes],
                (((1,), (1,)), ((), ())),
                precision=lax.Precision.HIGHEST,
                preferred_element_type=jnp.float32,
            )
        )
    stacked = jnp.concatenate(grads, axis=0)
    width = 2 * half
    col = lax.broadcasted_iota(jnp.int32, (rank, width), 1)
    row = lax.broadcasted_iota(jnp.int32, (rank, width), 0)
    colf = col.astype(jnp.float32)
    residue = colf - rank * jnp.floor((colf + 0.5) * (1.0 / rank))
    place = jnp.where(residue == row.astype(jnp.float32), 1.0, 0.0).astype(jnp.bfloat16)
    flat = None
    for term in split3(stacked):
        piece = jnp.dot(term, place, preferred_element_type=jnp.float32)
        flat = piece if flat is None else flat + piece
    keep = (col >= row * rank) & (col < row * rank + rank)
    id_col = lax.broadcasted_iota(jnp.int32, (1, width), 1) == round_up(size, NB)
    for s in range(ex_local):
        slot = jnp.where(keep, flat[s * rank : (s + 1) * rank], 0.0)
        line = jnp.sum(slot, axis=0, keepdims=True)
        line = jnp.where(id_col, jnp.broadcast_to(aux_ref[1:2, s : s + 1], line.shape), line)
        mine[s : s + 1, :] = line[:, 0:half]
        mine[ex_local + s : ex_local + s + 1, :] = line[:, half:width]
    copies = []
    for d in range(1, pieces):
        copy = pltpu.make_async_remote_copy(
            src_ref=mine,
            dst_ref=gathered.at[di],
            send_sem=dp_send.at[d - 1],
            recv_sem=dp_recv.at[d - 1],
            device_id=(lax.rem(di + d, pieces), ti),
            device_id_type=MESH,
        )
        copy.start()
        copies.append(copy)
    gathered[di] = mine[...]
    for copy in copies:
        copy.wait()
    for p in range(pieces):
        block = gathered[p]
        out_ref[p * ex_local : (p + 1) * ex_local, 0:half] = block[0:ex_local]
        out_ref[p * ex_local : (p + 1) * ex_local, half:width] = block[ex_local : 2 * ex_local]


def project(activations, out_grads, proj_in, proj_out, lengths, example_ids, queries):
    ex_local = lengths.shape[0]
    layers, tokens, _ = activations.shape
    rank = proj_in.shape[1]
    size = rank * rank
    width = round_up(size, CB)
    pieces = lax.axis_size("dp")
    seq_len = tokens // ex_local
    live = (jnp.arange(seq_len, dtype=jnp.int32)[None, :] < lengths[:, None]).astype(jnp.float32)
    ids = jnp.pad(example_ids.astype(jnp.float32), (0, tokens - ex_local))
    aux = jnp.stack([live.reshape(tokens), ids])
    return pl.pallas_call(
        functools.partial(project_kernel, ex_local, size),
        out_shape=jax.ShapeDtypeStruct((CB, width), jnp.float32),
        in_specs=[pl.BlockSpec(memory_space=pl.ANY)] * 2
        + [pl.BlockSpec(memory_space=pltpu.VMEM)] * 4,
        out_specs=pl.BlockSpec(memory_space=pltpu.VMEM),
        scratch_shapes=[
            pltpu.VMEM(activations.shape, activations.dtype),
            pltpu.VMEM(out_grads.shape, out_grads.dtype),
            pltpu.VMEM((layers, 2 * rank, tokens), jnp.float32),
            pltpu.VMEM((layers - 1, 2 * rank, tokens), jnp.float32),
            pltpu.VMEM((2 * ex_local, width // 2), jnp.float32),
            pltpu.VMEM((pieces, 2 * ex_local, width // 2), jnp.float32),
            pltpu.SemaphoreType.DMA((2 * layers,)),
            pltpu.SemaphoreType.DMA((layers - 1,)),
            pltpu.SemaphoreType.DMA((layers - 1,)),
            pltpu.SemaphoreType.DMA((pieces - 1,)),
            pltpu.SemaphoreType.DMA((pieces - 1,)),
        ],
        compiler_params=pltpu.CompilerParams(
            collective_id=0, has_side_effects=True, vmem_limit_bytes=48 * 1024 * 1024
        ),
    )(activations, out_grads, proj_in, proj_out, aux, queries)


def solve_scores(prior, damping, rhs, slots, asked, ex_local):
    size = prior.shape[0]
    width = rhs.shape[1]
    rows = width + rhs.shape[0]
    return pl.pallas_call(
        functools.partial(solve_kernel, size, slots, asked, ex_local),
        out_shape=jax.ShapeDtypeStruct((ex_local, asked), jnp.float32),
        in_specs=[
            pl.BlockSpec(memory_space=pltpu.SMEM),
            pl.BlockSpec(memory_space=pltpu.VMEM),
            pl.BlockSpec(memory_space=pltpu.VMEM),
        ],
        out_specs=pl.BlockSpec(memory_space=pltpu.VMEM),
        scratch_shapes=[
            pltpu.VMEM((rows // CB, rows, CB), jnp.float32),
            pltpu.VMEM((rows, TERMS * NB), jnp.bfloat16),
            pltpu.VMEM((rows, TERMS * NB), jnp.bfloat16),
            pltpu.VMEM((NB, NB), jnp.float32),
        ],
        compiler_params=pltpu.CompilerParams(vmem_limit_bytes=56 * 1024 * 1024),
    )(damping.reshape(1, 1), prior, rhs)


def per_device(
    activations, out_grads, proj_in, proj_out, lengths, example_ids, prior_cov, damping, queries
):
    ex_local = lengths.shape[0]
    slots = ex_local * lax.axis_size("dp")
    rhs = project(
        activations, out_grads, proj_in, proj_out, lengths, example_ids, queries[0]
    )
    chosen = solve_scores(prior_cov[0], damping, rhs, slots, queries.shape[1], ex_local)
    return lax.psum(chosen, "tensor")


def solution(mesh):
    in_specs = (
        P(None, "dp", "tensor"),
        P(None, "dp", "tensor"),
        P(None, None, "tensor"),
        P(None, None, "tensor"),
        P("dp"),
        P("dp"),
        P("tensor", None, None),
        P("tensor"),
        P("tensor", None, None),
    )
    out_specs = P("dp", None)
    return jax.shard_map(
        per_device, mesh=mesh, in_specs=in_specs, out_specs=out_specs, check_vma=False
    )
```
